32 devices in a mesh: group: 2 (over x), ctx: 16 (over z, y, core).
Axes of the slice: x: 2, y: 2, z: 4, core: 2. Of those that a mesh axis runs over, the one named last changes fastest.
Arguments:
- normed_hidden: bfloat16 [4096, 8192], P(('group', 'ctx')), parts along dimension 0, may hold values from -6 to 6
- queries: bfloat16 [4096, 4096], P(('group', 'ctx')), parts along dimension 0, may hold values from -45 to 45
- keys: bfloat16 [4096, 512], P(('group', 'ctx')), parts along dimension 0, may hold values from -6 to 6
- value_frozen_matrix: bfloat16 [8192, 512], P('ctx'), may hold values from -0.0625 to 0.0625
- adapter_down_weight: bfloat16 [8192, 64], replicated, may hold values from -0.0625 to 0.0625
- adapter_up_weight: bfloat16 [64, 512], replicated, may hold values from -0.75 to 0.75
- block_slot_index: int32 [64], P(('group', 'ctx')), parts along dimension 0, may hold values from 0 to 31, each once
Outputs:
- attended: bfloat16 [4096, 4096], P(('group', 'ctx')), parts along dimension 0
The draws below stay inside these ranges and needn't reach their ends.
There are 2 independent parts, one for each index of `group`. The reference program is written for one: setup_inputs(seed, part) draws one part's arguments, and reference() takes and returns one part's arrays. A program takes and returns all parts, laid end to end along the dimension named above; an argument that names none is the same for every part. Nothing has to cross between parts.
Inputs may be any that keep to these rules, and one draw needn't show every extreme that they name: `block_slot_index`: each of the 32 blocks is named once; slot j holds rows j*64 to (j+1)*64 - 1.
All inputs are finite; a program needn't handle non-finite values.
Results may differ from the reference program's by a relative error of at most 0.0054.
Values may be sent and summed in bfloat16 or wider, within the bound.
A program may use at most 192 MiB of HBM per device.

```python
import jax
import jax.numpy as jnp
from jax import lax

MODEL_WIDTH = 8192
QH = 32
KVH = 4
HD = 128
ADAPTER_RANK = 64
TOK_DEV = 128
BLK = 64
SEQ = 2048
NBLK = 32
G = 8
KEY_VALUE_WIDTH = 512
QW = 4096


def shared_fields(key):
    base_key = jax.random.fold_in(key, 11)
    key_a = jax.random.fold_in(base_key, 0)
    key_b = jax.random.fold_in(base_key, 1)
    key_d = jax.random.fold_in(base_key, 3)
    key_e = jax.random.fold_in(base_key, 4)
    base_q = jnp.clip(jax.random.normal(key_a, (SEQ, QH * HD), jnp.float32) * 2.5, -15.0, 15.0)
    base_k = jnp.clip(jax.random.normal(key_b, (SEQ, KVH * HD), jnp.float32), -6.0, 6.0)
    picked = jnp.zeros((SEQ,), dtype=bool)
    strength = jax.random.uniform(key_d, (SEQ, 1), jnp.float32, 8.0, 24.0)
    shrink = jax.random.uniform(key_e, (SEQ, 1), jnp.float32, 0.004, 0.012)
    repeated = jnp.repeat(base_k.reshape(SEQ, KVH, HD), QH // KVH, axis=1).reshape(SEQ, QH * HD)
    queries = jnp.where(picked[:, None], strength * repeated, base_q)
    next_k = jnp.roll(base_k, -1, axis=0)
    next_pick = jnp.roll(picked, -1)
    next_shrink = jnp.roll(shrink, -1, axis=0)
    keys = jnp.where(next_pick[:, None], next_k * (1.0 - next_shrink), base_k)
    return (queries, keys)


def draw_queries(key, part):
    return shared_fields(key)[0].astype(jnp.bfloat16)


def draw_keys(key, part):
    return shared_fields(key)[1].astype(jnp.bfloat16)


def block_scale(own_key, extent, cuts, least, largest):
    factor_of = 1.0
    for dim, parts in cuts:
        draws = jax.random.uniform(jax.random.fold_in(jax.random.fold_in(own_key, 6), dim), (parts,), jnp.float32, least / len(cuts), largest / len(cuts))
        factor_of = factor_of * jnp.repeat(jnp.exp(draws), extent[dim] // parts).reshape((-1,) + (1,) * (len(extent) - 1 - dim))
    return factor_of


def gaussian(rng, extent, width, reach, shards=(), kind=jnp.bfloat16):
    values = jax.random.normal(rng, extent, jnp.float32) * width
    if len(shards) > 0:
        values = block_scale(rng, extent, shards, -0.22, 0.18) * values
    return jnp.clip(values, min=-reach, max=reach).astype(kind)


def setup_inputs(seed: int = 0, part: int = 0) -> dict:
    streams_of = jax.random.split(jax.random.key(seed), 8)
    part_splits = jax.random.split(jax.random.fold_in(streams_of[7], part), 8)
    normed_hidden = gaussian(part_splits[0], (SEQ, MODEL_WIDTH), 1.0, 6.0, ((0, 16),))
    queries = draw_queries(jax.random.fold_in(jax.random.fold_in(streams_of[7], part), 71), part)
    keys = draw_keys(jax.random.fold_in(jax.random.fold_in(streams_of[7], part), 71), part)
    value_frozen_matrix = gaussian(streams_of[3], (MODEL_WIDTH, KEY_VALUE_WIDTH), MODEL_WIDTH ** -0.5, 0.0625, ((0, 16),))
    adapter_down_weight = gaussian(streams_of[4], (MODEL_WIDTH, ADAPTER_RANK), MODEL_WIDTH ** -0.5, 0.0625)
    adapter_up_weight = gaussian(streams_of[5], (ADAPTER_RANK, KEY_VALUE_WIDTH), ADAPTER_RANK ** -0.5, 0.75)
    block_slot_index = jax.random.permutation(part_splits[6], NBLK).astype(jnp.int32)
    return {"normed_hidden": normed_hidden, "queries": queries, "keys": keys, "value_frozen_matrix": value_frozen_matrix, "adapter_down_weight": adapter_down_weight, "adapter_up_weight": adapter_up_weight, "block_slot_index": block_slot_index}


def reference(normed_hidden, queries, keys, value_frozen_matrix, adapter_down_weight, adapter_up_weight, block_slot_index):
    offsets = jnp.arange(BLK, dtype=jnp.int32)
    positions = (block_slot_index[:, None].astype(jnp.int32) * BLK + offsets[None, :]).reshape(SEQ)
    frozen_output = jnp.dot(normed_hidden, value_frozen_matrix, preferred_element_type=jnp.float32)
    low_rank_output = jnp.dot(normed_hidden, adapter_down_weight, preferred_element_type=jnp.float32).astype(jnp.bfloat16)
    value_output = (frozen_output + 0.5 * jnp.dot(low_rank_output, adapter_up_weight, preferred_element_type=jnp.float32)).astype(jnp.bfloat16)
    keys_f = keys.astype(jnp.float32).reshape(SEQ, KVH, HD)
    values_f = value_output.astype(jnp.float32).reshape(SEQ, KVH, HD)
    scale = 1.0 / (HD ** 0.5)
    count = SEQ // TOK_DEV
    q_blocks = queries.reshape(count, TOK_DEV, QW)
    p_blocks = positions.reshape(count, TOK_DEV)

    def one_block(pair):
        q_blk, q_pos = pair
        q_f = q_blk.astype(jnp.float32).reshape(TOK_DEV, KVH, G, HD)
        scores = jnp.einsum("tkgd,skd->kgts", q_f, keys_f) * scale
        visible = (q_pos[:, None] >= positions[None, :])[None, None]
        scores = jnp.where(visible, scores, -1e30)
        top = jnp.max(scores, axis=-1, keepdims=True)
        weights = jnp.where(visible, jnp.exp(scores - top), 0.0)
        total = jnp.sum(weights, axis=-1)
        rounded = lax.optimization_barrier(weights.astype(jnp.bfloat16))
        summed = jnp.einsum("kgts,skd->kgtd", rounded.astype(jnp.float32), values_f)
        result = summed / total[..., None]
        return jnp.transpose(result, (2, 0, 1, 3)).reshape(TOK_DEV, QW).astype(jnp.bfloat16)

    return lax.map(one_block, (q_blocks, p_blocks)).reshape(SEQ, QW)
```

```python
import functools

import jax
import jax.numpy as jnp
from jax import lax
from jax.experimental import pallas as pl
from jax.experimental.pallas import tpu as pltpu
from jax.sharding import PartitionSpec as P

QH = 32
KVH = 4
HD = 128
BLK = 64


def shards(
    normed_hidden,
    queries,
    keys,
    value_frozen_matrix,
    adapter_down_weight,
    adapter_up_weight,
    block_slot_index,
):
    tokens = normed_hidden.shape[0]
    scale = 1.0 / HD**0.5
    offsets = jnp.arange(BLK, dtype=jnp.int32)
    table = lax.all_gather(block_slot_index, "ctx", axis=0, tiled=True)
    my_pos = (block_slot_index[:, None] * BLK + offsets[None, :]).reshape(tokens)
    frozen_output = jnp.dot(
        normed_hidden,
        lax.all_gather(value_frozen_matrix, "ctx", axis=0, tiled=True),
        preferred_element_type=jnp.float32,
    )
    low_rank_output = jnp.dot(
        normed_hidden, adapter_down_weight, preferred_element_type=jnp.float32
    ).astype(jnp.bfloat16)
    value_output = (
        frozen_output
        + 0.5 * jnp.dot(low_rank_output, adapter_up_weight, preferred_element_type=jnp.float32)
    ).astype(jnp.bfloat16)
    slots_here = tokens // BLK
    query_slots = [
        queries[which * BLK : (which + 1) * BLK].reshape(BLK, KVH, QH // KVH, HD)
        for which in range(slots_here)
    ]
    pos_slots = [my_pos[which * BLK : (which + 1) * BLK] for which in range(slots_here)]
    shape_stat = (KVH, QH // KVH, BLK)
    init = tuple(
        (
            (
                jnp.full(shape_stat, -1e30, jnp.float32),
                jnp.zeros(shape_stat, jnp.float32),
                jnp.zeros(shape_stat + (HD,), jnp.float32),
            )
            for which in range(slots_here)
        )
    )
    key_piece = lax.all_gather(keys, "ctx", axis=0, tiled=True)
    count = key_piece.shape[0]
    key_pos = (table[:, None] * BLK + offsets[None, :]).reshape(count)
    key_three = key_piece.reshape(count, KVH, HD)
    value_three = lax.all_gather(value_output, "ctx", axis=0, tiled=True).reshape(count, KVH, HD)
    lowest_key = jnp.min(key_pos)
    updated = []
    for attend_which in range(slots_here):
        q_part = query_slots[attend_which]
        q_pos = pos_slots[attend_which]

        def update(state, q_part=q_part, q_pos=q_pos):
            top, total, accum = state
            scores = (
                jnp.einsum("tkgd,skd->kgts", q_part, key_three, preferred_element_type=jnp.float32)
                * scale
            )
            visible = (q_pos[:, None] >= key_pos[None, :])[None, None]
            scores = jnp.where(visible, scores, -1e30)
            top_new = jnp.maximum(top, jnp.max(scores, axis=-1))
            weights = jnp.where(visible, jnp.exp(scores - top_new[..., None]), 0.0)
            total = jnp.sum(weights, axis=-1)
            accum = jnp.einsum(
                "kgts,skd->kgtd",
                weights.astype(jnp.bfloat16),
                value_three,
                preferred_element_type=jnp.float32,
            )
            return (top_new, total, accum)

        def keep(state):
            return state

        updated.append(lax.cond(lowest_key <= jnp.max(q_pos), update, keep, init[attend_which]))
    states = tuple(updated)
    outputs = []
    for which in range(slots_here):
        result = states[which][2] / states[which][1][..., None]
        outputs.append(
            jnp.transpose(result, (2, 0, 1, 3)).reshape(BLK, QH * HD).astype(jnp.bfloat16)
        )
    return jnp.concatenate(outputs, axis=0)


NZ = 4
NC = 2
G = QH // KVH
NSLOT = 4 * NZ
HU = 2


def fused_kernel(
    slot_ref, hid_ref, q_ref, k_ref, w_ref, down_ref, up_ref, out_ref,
    kbuf, vbuf, wbuf, hall, psend, precv, wts, recip, bias,
    k_ss, k_rs, w_ss, w_rs, h_ss, h_rs, p_ss, p_rs, v_ss, v_rs,
):
    f32, bf16 = jnp.float32, jnp.bfloat16
    x = lax.axis_index("group")
    me = lax.axis_index("ctx")
    z, y, c = me // 4, (me // 2) % 2, me % 2
    tokens = k_ref.shape[0]
    half = w_ref.shape[0] // 2
    cols = w_ref.shape[1] // NC
    hpc = QH // NC

    def at(gx, zz, yy, cc):
        return (gx, zz * 4 + yy * 2 + cc)

    z_peer = {d: at(x, (z + d) % NZ, y, c) for d in range(1, NZ)}
    y_peer = at(x, z, 1 - y, c)
    c_peer = at(x, z, y, 1 - c)
    p_peer = [None, at(x, z, y, 1 - c), at(1 - x, z, y, c), at(1 - x, z, y, 1 - c)]
    started = []

    def remote(src, dst, ss, rs, peer):
        return pltpu.make_async_remote_copy(
            src_ref=src, dst_ref=dst, send_sem=ss, recv_sem=rs,
            device_id=peer, device_id_type=pl.DeviceIdType.MESH,
        )

    def go(copy):
        copy.start()
        started.append(copy)
        return copy

    b0 = slot_ref[0].astype(f32)
    b1 = slot_ref[1].astype(f32)
    kbuf[0, :tokens, :] = k_ref[...]
    lane = lax.broadcasted_iota(jnp.int32, (16, k_ref.shape[1]), 1) % tokens
    kbuf[0, tokens:, :] = jnp.where(lane < BLK, b0, b1).astype(bf16)

    barrier = pltpu.get_barrier_semaphore()
    peers = list(z_peer.values()) + [y_peer] + p_peer[1:]
    for peer in peers:
        pl.semaphore_signal(barrier, inc=1, device_id=peer, device_id_type=pl.DeviceIdType.MESH)
    pl.semaphore_wait(barrier, len(peers))

    def gather(src0, view, ss, rs, pair=True):
        zc = {d: remote(src0, view(NZ - d), ss(d - 1), rs(d - 1), z_peer[d]) for d in range(1, NZ)}
        yc = {}
        cc = {}
        for j in range(NZ):
            yc[j] = remote(src0 if j == 0 else view(j), view(4 + j), ss(3 + j), rs(3 + j), y_peer)
        for j in range(2 * NZ if pair else 0):
            cc[j] = remote(src0 if j == 0 else view(j), view(8 + j), ss(7 + j), rs(7 + j), c_peer)
        return zc, yc, cc

    kz, ky, kc = gather(kbuf.at[0], lambda s: kbuf.at[s], lambda i: k_ss.at[i], lambda i: k_rs.at[i])
    for d in range(1, NZ):
        go(kz[d])
    go(ky[0])
    go(kc[0])

    def column(j, cc, xx):
        dz, dy = j % NZ, j // NZ
        block = at(0, (z + dz) % NZ, (y + dy) % 2, cc)[1]
        return pl.multiple_of(block * (2 * half) + xx * half, half)

    hc = {}
    for p in (2, 3, 1):
        px, pc = (x, 1 - x)[p // 2], (c, 1 - c)[p % 2]
        for j in range(2 * NZ):
            hc[p, j] = go(remote(
                hid_ref.at[:, pl.ds(column(j, pc, px), half)],
                hall.at[pl.ds(p * tokens, tokens), pl.ds(j * half, half)],
                h_ss.at[p - 1, j], h_rs.at[p - 1, j], p_peer[p],
            ))

    row0 = pl.multiple_of(x * half, half)
    wz, wy = [], []
    for ch in range(NC):
        wbuf[ch, :half, :] = w_ref[pl.ds(row0, half), ch * cols:(ch + 1) * cols]
        zc, yc, _ = gather(
            wbuf.at[ch, pl.ds(0, half)],
            lambda s, ch=ch: wbuf.at[ch, pl.ds((s % 8) * half, half)],
            lambda i, ch=ch: w_ss.at[ch, i], lambda i, ch=ch: w_rs.at[ch, i], pair=False,
        )
        wz.append(zc)
        wy.append(yc)

    def w_send(ch):
        for d in range(1, NZ):
            go(wz[ch][d])
        go(wy[ch][0])

    def z_forward(zc, yc, cc=None):
        for d in (1, 3, 2):
            zc[d].wait_recv()
            go(yc[NZ - d])
            if cc is not None:
                go(cc[NZ - d])

    def y_forward(yc, cc):
        for j in range(NZ):
            yc[j].wait_recv()
            go(cc[NZ + j])

    w_send(0)
    low = jnp.dot(hid_ref[...], down_ref[...], preferred_element_type=f32).astype(bf16)
    for j in range(2 * NZ):
        hall[:tokens, j * half:(j + 1) * half] = hid_ref[:, pl.ds(column(j, c, x), half)]
    adapter = 0.5 * jnp.dot(low, up_ref[...], preferred_element_type=f32)

    z_forward(kz, ky, kc)
    y_forward(ky, kc)
    z_forward(wz[0], wy[0])
    w_send(1)
    for j in range(2 * NZ):
        kc[j].wait_recv()

    row = lax.broadcasted_iota(jnp.int32, (tokens, tokens), 0)
    col = lax.broadcasted_iota(jnp.int32, (tokens, tokens), 1)
    q_pos = jnp.where(row < BLK, b0, b1) * BLK + (row % BLK).astype(f32)
    for s in range(NSLOT):
        blocks = kbuf[s, tokens:, :tokens].astype(f32)[0:1]
        k_pos = blocks * BLK + (col % BLK).astype(f32)
        bias[:, s * tokens:(s + 1) * tokens] = jnp.where(q_pos >= k_pos, 0.0, -1e30)

    rate = 1.4426950408889634 / HD**0.5
    count = NSLOT * tokens

    def softmax(first, last):
        for g in range(KVH):
            lo, hi = max(first, g * G), min(last, (g + 1) * G)
            if lo >= hi:
                continue

            @pl.loop(lo // HU, hi // HU)
            def _(u, g=g):
                keys = kbuf[:, :tokens, g * HD:(g + 1) * HD].reshape(count, HD)
                q = jnp.concatenate(
                    [q_ref[:, pl.ds(pl.multiple_of((u * HU + i) * HD, HD), HD)] for i in range(HU)], axis=0
                )
                s = lax.dot_general(q, keys, (((1,), (1,)), ((), ())), preferred_element_type=f32)
                s = s.reshape(HU, tokens, count) + bias[...][None]
                top = jnp.max(s, axis=-1, keepdims=True)
                e = jnp.exp2((s - top) * rate)
                total = jnp.sum(e, axis=-1, keepdims=True)
                wts[pl.ds(u * HU, HU)] = e.astype(bf16)
                recip[pl.ds(u * HU, HU)] = jnp.broadcast_to(1.0 / total, (HU, tokens, HD))

    pc = {}
    vz, vy, vc = [], [], []
    for ch in range(NC):
        zc, yc, cc = gather(
            vbuf.at[0, :, pl.ds(ch * cols, cols)],
            lambda s, ch=ch: vbuf.at[s, :, pl.ds(ch * cols, cols)],
            lambda i, ch=ch: v_ss.at[ch, i], lambda i, ch=ch: v_rs.at[ch, i],
        )
        vz.append(zc)
        vy.append(yc)
        vc.append(cc)
    own = {}

    def partial(ch):
        acc = jnp.dot(hall[...], wbuf[ch], preferred_element_type=f32)
        for p in (3, 2, 1):
            psend[ch, p - 1] = acc[p * tokens:(p + 1) * tokens].astype(bf16)
            pc[ch, p] = go(remote(
                psend.at[ch, p - 1], precv.at[ch, p - 1], p_ss.at[ch, p - 1], p_rs.at[ch, p - 1], p_peer[p]
            ))
        own[ch] = acc[:tokens] + adapter[:, ch * cols:(ch + 1) * cols]

    def values(ch):
        acc = own[ch]
        for p in (1, 2, 3):
            pc[ch, p].wait_recv()
            acc = acc + precv[ch, p - 1].astype(f32)
        vbuf[0, :, ch * cols:(ch + 1) * cols] = acc.astype(bf16)
        for d in range(1, NZ):
            go(vz[ch][d])
        go(vy[ch][0])
        go(vc[ch][0])

    def attend(ch):
        for g in range(ch * KVH // NC, (ch + 1) * KVH // NC):
            @pl.loop(g * G // HU, (g + 1) * G // HU)
            def _(u, g=g):
                v = vbuf[:, :, g * HD:(g + 1) * HD].reshape(count, HD)
                w = wts[pl.ds(u * HU, HU)].reshape(HU * tokens, count)
                o = jnp.dot(w, v, preferred_element_type=f32)
                for i in range(HU):
                    r = o[i * tokens:(i + 1) * tokens] * recip[u * HU + i]
                    out_ref[:, pl.ds(pl.multiple_of((u * HU + i) * HD, HD), HD)] = r.astype(bf16)

    softmax(0, 6)
    z_forward(wz[1], wy[1])
    softmax(6, 12)
    for copy in hc.values():
        copy.wait_recv()
    for j in range(NZ):
        wy[0][j].wait_recv()
    partial(0)
    softmax(12, 18)
    values(0)
    for j in range(NZ):
        wy[1][j].wait_recv()
    partial(1)
    softmax(18, 24)
    z_forward(vz[0], vy[0], vc[0])
    values(1)
    softmax(24, 32)
    y_forward(vy[0], vc[0])
    z_forward(vz[1], vy[1], vc[1])
    for j in range(2 * NZ):
        vc[0][j].wait_recv()
    attend(0)
    y_forward(vy[1], vc[1])
    for j in range(2 * NZ):
        vc[1][j].wait_recv()
    attend(1)
    for copy in started:
        copy.wait_send()


def fused_shards(
    normed_hidden,
    queries,
    keys,
    value_frozen_matrix,
    adapter_down_weight,
    adapter_up_weight,
    block_slot_index,
):
    tokens, width = keys.shape
    rows = value_frozen_matrix.shape[0]
    cols = width // NC
    bf16 = jnp.bfloat16
    vmem = pl.BlockSpec(memory_space=pltpu.VMEM)
    dma = pltpu.SemaphoreType.DMA
    return pl.pallas_call(
        fused_kernel,
        out_shape=jax.ShapeDtypeStruct(queries.shape, bf16),
        in_specs=[pl.BlockSpec(memory_space=pltpu.SMEM)] + [vmem] * 6,
        out_specs=vmem,
        scratch_shapes=[
            pltpu.VMEM((NSLOT, tokens + 16, width), bf16),
            pltpu.VMEM((NSLOT, tokens, width), bf16),
            pltpu.VMEM((NC, 4 * rows, cols), bf16),
            pltpu.VMEM((4 * tokens, 4 * rows), bf16),
            pltpu.VMEM((NC, 3, tokens, cols), bf16),
            pltpu.VMEM((NC, 3, tokens, cols), bf16),
            pltpu.VMEM((QH, tokens, NSLOT * tokens), bf16),
            pltpu.VMEM((QH, tokens, HD), jnp.float32),
            pltpu.VMEM((tokens, NSLOT * tokens), jnp.float32),
            dma((15,)), dma((15,)),
            dma((NC, 7)), dma((NC, 7)),
            dma((3, 8)), dma((3, 8)),
            dma((NC, 3)), dma((NC, 3)),
            dma((NC, 15)), dma((NC, 15)),
        ],
        compiler_params=pltpu.CompilerParams(
            collective_id=0, has_side_effects=True, vmem_limit_bytes=56 * 2**20
        ),
        cost_estimate=pl.CostEstimate(flops=6 * 10**9, bytes_accessed=8 * 10**6, transcendentals=8 * 10**6),
    )(
        block_slot_index, normed_hidden, queries, keys,
        value_frozen_matrix, adapter_down_weight, adapter_up_weight,
    )


def solution(mesh):
    in_specs = (
        P(("group", "ctx"), None),
        P(("group", "ctx"), None),
        P(("group", "ctx"), None),
        P("ctx", None),
        P(),
        P(),
        P(("group", "ctx")),
    )
    out_specs = P(("group", "ctx"), None)
    body = fused_shards if mesh.shape["ctx"] == 4 * NZ and mesh.shape["group"] == 2 else shards
    return jax.shard_map(body, mesh=mesh, in_specs=in_specs, out_specs=out_specs, check_vma=False)
```

```python
import functools

import jax
import jax.numpy as jnp
from jax import lax
from jax.experimental import pallas as pl
from jax.experimental.pallas import tpu as pltpu
from jax.sharding import PartitionSpec as P

QH = 32
KVH = 4
HD = 128
BLK = 64


def shards(
    normed_hidden,
    queries,
    keys,
    value_frozen_matrix,
    adapter_down_weight,
    adapter_up_weight,
    block_slot_index,
):
    tokens = normed_hidden.shape[0]
    scale = 1.0 / HD**0.5
    offsets = jnp.arange(BLK, dtype=jnp.int32)
    table = lax.all_gather(block_slot_index, "ctx", axis=0, tiled=True)
    my_pos = (block_slot_index[:, None] * BLK + offsets[None, :]).reshape(tokens)
    frozen_output = jnp.dot(
        normed_hidden,
        lax.all_gather(value_frozen_matrix, "ctx", axis=0, tiled=True),
        preferred_element_type=jnp.float32,
    )
    low_rank_output = jnp.dot(
        normed_hidden, adapter_down_weight, preferred_element_type=jnp.float32
    ).astype(jnp.bfloat16)
    value_output = (
        frozen_output
        + 0.5 * jnp.dot(low_rank_output, adapter_up_weight, preferred_element_type=jnp.float32)
    ).astype(jnp.bfloat16)
    slots_here = tokens // BLK
    query_slots = [
        queries[which * BLK : (which + 1) * BLK].reshape(BLK, KVH, QH // KVH, HD)
        for which in range(slots_here)
    ]
    pos_slots = [my_pos[which * BLK : (which + 1) * BLK] for which in range(slots_here)]
    shape_stat = (KVH, QH // KVH, BLK)
    init = tuple(
        (
            (
                jnp.full(shape_stat, -1e30, jnp.float32),
                jnp.zeros(shape_stat, jnp.float32),
                jnp.zeros(shape_stat + (HD,), jnp.float32),
            )
            for which in range(slots_here)
        )
    )
    key_piece = lax.all_gather(keys, "ctx", axis=0, tiled=True)
    count = key_piece.shape[0]
    key_pos = (table[:, None] * BLK + offsets[None, :]).reshape(count)
    key_three = key_piece.reshape(count, KVH, HD)
    value_three = lax.all_gather(value_output, "ctx", axis=0, tiled=True).reshape(count, KVH, HD)
    lowest_key = jnp.min(key_pos)
    updated = []
    for attend_which in range(slots_here):
        q_part = query_slots[attend_which]
        q_pos = pos_slots[attend_which]

        def update(state, q_part=q_part, q_pos=q_pos):
            top, total, accum = state
            scores = (
                jnp.einsum("tkgd,skd->kgts", q_part, key_three, preferred_element_type=jnp.float32)
                * scale
            )
            visible = (q_pos[:, None] >= key_pos[None, :])[None, None]
            scores = jnp.where(visible, scores, -1e30)
            top_new = jnp.maximum(top, jnp.max(scores, axis=-1))
            weights = jnp.where(visible, jnp.exp(scores - top_new[..., None]), 0.0)
            total = jnp.sum(weights, axis=-1)
            accum = jnp.einsum(
                "kgts,skd->kgtd",
                weights.astype(jnp.bfloat16),
                value_three,
                preferred_element_type=jnp.float32,
            )
            return (top_new, total, accum)

        def keep(state):
            return state

        updated.append(lax.cond(lowest_key <= jnp.max(q_pos), update, keep, init[attend_which]))
    states = tuple(updated)
    outputs = []
    for which in range(slots_here):
        result = states[which][2] / states[which][1][..., None]
        outputs.append(
            jnp.transpose(result, (2, 0, 1, 3)).reshape(BLK, QH * HD).astype(jnp.bfloat16)
        )
    return jnp.concatenate(outputs, axis=0)


NZ = 4
NC = 4
AHEAD = 4
G = QH // KVH
NSLOT = 4 * NZ
HU = 2
HA = 4


def fused_kernel(
    slot_ref, hid_hbm, q_hbm, k_ref, w_ref, down_hbm, up_ref, out_ref,
    kbuf, vbuf, wbuf, hall, psend, precv, wts, recip, bias, hid_ref, q_ref, down_ref, load_sem,
    k_ss, k_rs, w_ss, w_rs, h_ss, h_rs, p_ss, p_rs, v_ss, v_rs,
):
    f32, bf16 = jnp.float32, jnp.bfloat16
    x = lax.axis_index("group")
    me = lax.axis_index("ctx")
    z, y, c = me // 4, (me // 2) % 2, me % 2
    tokens = k_ref.shape[0]
    half = w_ref.shape[0] // 2
    cols = w_ref.shape[1] // NC
    hpc = QH // NC

    def at(gx, zz, yy, cc):
        return (gx, zz * 4 + yy * 2 + cc)

    z_peer = {d: at(x, (z + d) % NZ, y, c) for d in range(1, NZ)}
    y_peer = at(x, z, 1 - y, c)
    c_peer = at(x, z, y, 1 - c)
    p_peer = [None, at(x, z, y, 1 - c), at(1 - x, z, y, c), at(1 - x, z, y, 1 - c)]
    started = []

    def remote(src, dst, ss, rs, peer):
        return pltpu.make_async_remote_copy(
            src_ref=src, dst_ref=dst, send_sem=ss, recv_sem=rs,
            device_id=peer, device_id_type=pl.DeviceIdType.MESH,
        )

    def go(copy):
        copy.start()
        started.append(copy)
        return copy

    loads = [
        pltpu.make_async_copy(src, dst, load_sem.at[i])
        for i, (src, dst) in enumerate(((down_hbm, down_ref), (hid_hbm, hid_ref), (q_hbm, q_ref)))
    ]
    b0 = slot_ref[0].astype(f32)
    b1 = slot_ref[1].astype(f32)
    for g in range(KVH):
        kbuf[g, 0, :tokens, :] = k_ref[:, g * HD:(g + 1) * HD]
    lane = lax.broadcasted_iota(jnp.int32, (16, HD), 1)
    kbuf[0, 0, tokens:, :] = jnp.where(lane < BLK, b0, b1).astype(bf16)

    barrier = pltpu.get_barrier_semaphore()
    peers = list(z_peer.values()) + [y_peer] + p_peer[1:]
    for peer in peers:
        pl.semaphore_signal(barrier, inc=1, device_id=peer, device_id_type=pl.DeviceIdType.MESH)
    pl.semaphore_wait(barrier, len(peers))

    def gather(src0, view, ss, rs, pair=True):
        zc = {d: remote(src0, view(NZ - d), ss(d - 1), rs(d - 1), z_peer[d]) for d in range(1, NZ)}
        yc = {}
        cc = {}
        for j in range(NZ):
            yc[j] = remote(src0 if j == 0 else view(j), view(4 + j), ss(3 + j), rs(3 + j), y_peer)
        for j in range(2 * NZ if pair else 0):
            cc[j] = remote(src0 if j == 0 else view(j), view(8 + j), ss(7 + j), rs(7 + j), c_peer)
        return zc, yc, cc

    queue, front = [], [0, 0]

    def enqueue(zc, yc, cc):
        for i, d in enumerate((1, 3, 2)):
            first = ([yc[0]] + ([cc[0]] if cc else [])) if i == 0 else []
            queue.append((zc[d], yc[NZ - d], cc.get(NZ - d), first))

    def launch(n):
        for item in queue[front[0]:front[0] + n]:
            for copy in item[3]:
                go(copy)
            go(item[0])
        front[0] = min(front[0] + n, len(queue))

    def pump(n):
        for item in queue[front[1]:front[1] + n]:
            item[0].wait_recv()
            go(item[1])
            if item[2] is not None:
                go(item[2])
            launch(1)
        front[1] += n

    kz, ky, kc = [], [], []
    for g in range(KVH):
        sent = pl.ds(0, tokens + 16 if g == 0 else tokens)
        zc, yc, cc = gather(
            kbuf.at[g, 0, sent],
            lambda s, g=g, sent=sent: kbuf.at[g, s, sent],
            lambda i, g=g: k_ss.at[g, i], lambda i, g=g: k_rs.at[g, i],
        )
        kz.append(zc)
        ky.append(yc)
        kc.append(cc)
    enqueue(kz[0], ky[0], kc[0])
    enqueue(kz[1], ky[1], kc[1])
    launch(3)

    def column(j, cc, xx):
        dz, dy = j % NZ, j // NZ
        block = at(0, (z + dz) % NZ, (y + dy) % 2, cc)[1]
        return pl.multiple_of(block * (2 * half) + xx * half, half)

    hc = {}
    for p in (2, 3, 1):
        px, pc = (x, 1 - x)[p // 2], (c, 1 - c)[p % 2]
        for j in range(2 * NZ):
            hc[p, j] = go(remote(
                hid_hbm.at[:, pl.ds(column(j, pc, px), half)],
                hall.at[pl.ds(p * tokens, tokens), pl.ds(j * half, half)],
                h_ss.at[p - 1, j], h_rs.at[p - 1, j], p_peer[p],
            ))

    row0 = pl.multiple_of(x * half, half)
    wy = []
    for ch in range(NC):
        wbuf[ch, :half, :] = w_ref[pl.ds(row0, half), ch * cols:(ch + 1) * cols]
        zc, yc, _ = gather(
            wbuf.at[ch, pl.ds(0, half)],
            lambda s, ch=ch: wbuf.at[ch, pl.ds((s % 8) * half, half)],
            lambda i, ch=ch: w_ss.at[ch, i], lambda i, ch=ch: w_rs.at[ch, i], pair=False,
        )
        enqueue(zc, yc, {})
        wy.append(yc)
        if ch >= 2:
            enqueue(kz[ch], ky[ch], kc[ch])

    launch(AHEAD - 3)

    def z_forward(zc, yc, cc=None):
        for d in (1, 3, 2):
            zc[d].wait_recv()
            go(yc[NZ - d])
            if cc is not None:
                go(cc[NZ - d])

    def y_forward(yc, cc):
        for j in range(NZ):
            yc[j].wait_recv()
            go(cc[NZ + j])

    for copy in loads:
        copy.start()
    pump(3)
    loads[1].wait()
    for j in range(2 * NZ):
        hall[:tokens, j * half:(j + 1) * half] = hid_ref[:, pl.ds(column(j, c, x), half)]
    pump(3)
    y_forward(ky[0], kc[0])
    loads[0].wait()
    low = lax.dot_general(
        hid_ref[...], down_ref[...], (((1,), (1,)), ((), ())), preferred_element_type=f32
    ).astype(bf16)
    adapter = 0.5 * jnp.dot(low, up_ref[...], preferred_element_type=f32)

    def k_wait(g):
        for j in range(2 * NZ):
            kc[g][j].wait_recv()

    k_wait(0)
    pump(1)

    row = lax.broadcasted_iota(jnp.int32, (tokens, tokens), 0)
    col = lax.broadcasted_iota(jnp.int32, (tokens, tokens), 1)
    q_pos = jnp.where(row < BLK, b0, b1) * BLK + (row % BLK).astype(f32)
    for s in range(NSLOT):
        blocks = kbuf[0, s, tokens:, :].astype(f32)[0:1]
        k_pos = blocks * BLK + (col % BLK).astype(f32)
        bias[:, s * tokens:(s + 1) * tokens] = jnp.where(q_pos >= k_pos, 0.0, -1e30)

    rate = 1.4426950408889634 / HD**0.5
    count = NSLOT * tokens

    def softmax(first, last):
        for g in range(KVH):
            lo, hi = max(first, g * G), min(last, (g + 1) * G)
            if lo >= hi:
                continue

            @pl.loop(lo // HU, hi // HU)
            def _(u, g=g):
                keys = kbuf[g, :, :tokens, :].reshape(count, HD)
                q = jnp.concatenate(
                    [q_ref[:, pl.ds(pl.multiple_of((u * HU + i) * HD, HD), HD)] for i in range(HU)], axis=0
                )
                s = lax.dot_general(q, keys, (((1,), (1,)), ((), ())), preferred_element_type=f32)
                s = s.reshape(HU, tokens, count) + bias[...][None]
                top = jnp.max(s, axis=-1, keepdims=True)
                e = jnp.exp2((s - top) * rate)
                total = jnp.sum(e, axis=-1, keepdims=True)
                wts[pl.ds(u * HU, HU)] = e.astype(bf16)
                recip[pl.ds(u * HU, HU)] = jnp.broadcast_to(1.0 / total, (HU, tokens, HD))

    pc = {}
    vz, vy, vc = [], [], []
    for ch in range(NC):
        zc, yc, cc = gather(
            vbuf.at[ch, 0],
            lambda s, ch=ch: vbuf.at[ch, s],
            lambda i, ch=ch: v_ss.at[ch, i], lambda i, ch=ch: v_rs.at[ch, i],
        )
        vz.append(zc)
        vy.append(yc)
        vc.append(cc)
    own = {}

    def partial(ch):
        acc = jnp.dot(hall[...], wbuf[ch], preferred_element_type=f32)
        for p in (3, 2, 1):
            psend[ch, p - 1] = acc[p * tokens:(p + 1) * tokens].astype(bf16)
            pc[ch, p] = go(remote(
                psend.at[ch, p - 1], precv.at[ch, p - 1], p_ss.at[ch, p - 1], p_rs.at[ch, p - 1], p_peer[p]
            ))
        own[ch] = acc[:tokens] + adapter[:, ch * cols:(ch + 1) * cols]

    def values(ch):
        acc = own[ch]
        for p in (1, 2, 3):
            pc[ch, p].wait_recv()
            acc = acc + precv[ch, p - 1].astype(f32)
        vbuf[ch, 0] = acc.astype(bf16)
        for d in range(1, NZ):
            go(vz[ch][d])
        go(vy[ch][0])
        go(vc[ch][0])

    def attend(ch):
        for g in range(ch * KVH // NC, (ch + 1) * KVH // NC):
            @pl.loop(g * G // HA, (g + 1) * G // HA)
            def _(u, g=g):
                v = vbuf[ch, :, :, (g * HD) % cols:(g * HD) % cols + HD].reshape(count, HD)
                w = wts[pl.ds(u * HA, HA)].reshape(HA * tokens, count)
                o = jnp.dot(w, v, preferred_element_type=f32)
                for i in range(HA):
                    r = o[i * tokens:(i + 1) * tokens] * recip[u * HA + i]
                    out_ref[:, pl.ds(pl.multiple_of((u * HA + i) * HD, HD), HD)] = r.astype(bf16)

    def w_wait(ch):
        for j in range(NZ):
            wy[ch][j].wait_recv()

    def v_wait(ch):
        for j in range(2 * NZ):
            vc[ch][j].wait_recv()

    loads[2].wait()
    softmax(0, 4)
    pump(2)
    y_forward(ky[1], kc[1])
    softmax(4, 8)
    pump(3)
    k_wait(1)
    softmax(8, 12)
    pump(3)
    softmax(12, 14)
    for copy in hc.values():
        copy.wait_recv()
    w_wait(0)
    partial(0)
    pump(3)
    w_wait(1)
    partial(1)
    values(0)
    softmax(14, 16)
    pump(3)
    z_forward(vz[0], vy[0], vc[0])
    w_wait(2)
    partial(2)
    values(1)
    y_forward(ky[2], kc[2])
    pump(3)
    z_forward(vz[1], vy[1], vc[1])
    k_wait(2)
    softmax(16, 18)
    w_wait(3)
    partial(3)
    values(2)
    y_forward(vy[0], vc[0])
    softmax(18, 22)
    values(3)
    z_forward(vz[2], vy[2], vc[2])
    y_forward(ky[3], kc[3])
    y_forward(vy[1], vc[1])
    softmax(22, 24)
    z_forward(vz[3], vy[3], vc[3])
    k_wait(3)
    softmax(24, 28)
    y_forward(vy[2], vc[2])
    softmax(28, 32)
    y_forward(vy[3], vc[3])
    for ch in range(NC):
        v_wait(ch)
        attend(ch)
    for copy in started:
        copy.wait_send()


def fused_shards(
    normed_hidden,
    queries,
    keys,
    value_frozen_matrix,
    adapter_down_weight,
    adapter_up_weight,
    block_slot_index,
):
    tokens, width = keys.shape
    rows = value_frozen_matrix.shape[0]
    cols = width // NC
    bf16 = jnp.bfloat16
    vmem = pl.BlockSpec(memory_space=pltpu.VMEM)
    hbm = pl.BlockSpec(memory_space=pl.ANY)
    dma = pltpu.SemaphoreType.DMA
    return pl.pallas_call(
        fused_kernel,
        out_shape=jax.ShapeDtypeStruct(queries.shape, bf16),
        in_specs=[pl.BlockSpec(memory_space=pltpu.SMEM), hbm, hbm, vmem, vmem, hbm, vmem],
        out_specs=vmem,
        scratch_shapes=[
            pltpu.VMEM((KVH, NSLOT, tokens + 16, HD), bf16),
            pltpu.VMEM((NC, NSLOT, tokens, cols), bf16),
            pltpu.VMEM((NC, 4 * rows, cols), bf16),
            pltpu.VMEM((4 * tokens, 4 * rows), bf16),
            pltpu.VMEM((NC, 3, tokens, cols), bf16),
            pltpu.VMEM((NC, 3, tokens, cols), bf16),
            pltpu.VMEM((QH, tokens, NSLOT * tokens), bf16),
            pltpu.VMEM((QH, tokens, HD), jnp.float32),
            pltpu.VMEM((tokens, NSLOT * tokens), jnp.float32),
            pltpu.VMEM(normed_hidden.shape, bf16),
            pltpu.VMEM(queries.shape, bf16),
            pltpu.VMEM(adapter_down_weight.shape[::-1], bf16),
            dma((3,)),
            dma((KVH, 15)), dma((KVH, 15)),
            dma((NC, 7)), dma((NC, 7)),
            dma((3, 8)), dma((3, 8)),
            dma((NC, 3)), dma((NC, 3)),
            dma((NC, 15)), dma((NC, 15)),
        ],
        compiler_params=pltpu.CompilerParams(
            collective_id=0, has_side_effects=True, vmem_limit_bytes=56 * 2**20
        ),
        cost_estimate=pl.CostEstimate(flops=6 * 10**9, bytes_accessed=8 * 10**6, transcendentals=8 * 10**6),
    )(
        block_slot_index, normed_hidden, queries, keys,
        value_frozen_matrix, adapter_down_weight.T, adapter_up_weight,
    )


def solution(mesh):
    in_specs = (
        P(("group", "ctx"), None),
        P(("group", "ctx"), None),
        P(("group", "ctx"), None),
        P("ctx", None),
        P(),
        P(),
        P(("group", "ctx")),
    )
    out_specs = P(("group", "ctx"), None)
    body = fused_shards if mesh.shape["ctx"] == 4 * NZ and mesh.shape["group"] == 2 else shards
    return jax.shard_map(body, mesh=mesh, in_specs=in_specs, out_specs=out_specs, check_vma=False)
```
